32 devices in a mesh: dp: 4 (over z), tensor: 4 (over y, x), section: 2 (over core).
Axes of the slice: x: 2, y: 2, z: 4, core: 2. Of those that a mesh axis runs over, the one named last changes fastest.
Arguments:
- grad_mat: bfloat16 [4, 4, 1600, 4800], P('dp', 'tensor', 'section'), may hold values from -6 to 6
- grad_vec: bfloat16 [4, 20800], P('dp'), may hold values from -6 to 6
- master_mat: float32 [4, 2, 4, 200, 4800], P('tensor', 'section', 'dp'), may hold values from -9 to 9
- first_mat: float32 [4, 2, 4, 200, 4800], P('tensor', 'section', 'dp'), may hold values from -4 to 4
- second_mat: float32 [4, 2, 4, 200, 4800], P('tensor', 'section', 'dp'), may hold values from 0.001 to 0.1
- master_vec: float32 [4, 5200], P('dp'), may hold values from -6 to 6
- first_vec: float32 [4, 5200], P('dp'), may hold values from -4 to 4
- second_vec: float32 [4, 5200], P('dp'), may hold values from 0.001 to 0.1
Outputs:
- weights_mat: bfloat16 [4, 1600, 4800], P('tensor', 'section')
- weights_vec: bfloat16 [20800], replicated
- new_master_mat: float32 [4, 2, 4, 200, 4800], P('tensor', 'section', 'dp')
- new_first_mat: float32 [4, 2, 4, 200, 4800], P('tensor', 'section', 'dp')
- new_second_mat: float32 [4, 2, 4, 200, 4800], P('tensor', 'section', 'dp')
- new_master_vec: float32 [4, 5200], P('dp')
- new_first_vec: float32 [4, 5200], P('dp')
- new_second_vec: float32 [4, 5200], P('dp')
The draws below stay inside these ranges and needn't reach their ends.
All inputs are finite; a program needn't handle non-finite values.
Results may differ from the reference program's by a relative error of at most 0.0004.
Values may be sent and summed in bfloat16 or wider, within the bound.
A program may use at most 128 MiB of HBM per device.

```python
import math
import jax
import jax.numpy as jnp
from jax import lax

D = 1600
FF = 6400
STEP = 10
COLS = 4800
OWNED_ROWS = 200
VECTOR = 20800
OWNED_VECTOR = 5200
N_DP = 4
N_TENSOR = 4
N_SECTION = 2


def draw_master_mat(key, part):
    key_base, key_rows, key_cols = jax.random.split(jax.random.fold_in(key, 11), 3)
    shape = (N_TENSOR, N_SECTION, N_DP, OWNED_ROWS, COLS)
    base = jnp.clip(jax.random.normal(key_base, shape, jnp.float32), -5.0, 5.0)
    row_scale = jnp.exp(math.log(10.0) * jax.random.uniform(key_rows, (N_TENSOR, N_SECTION, N_DP, OWNED_ROWS, 1), jnp.float32))
    col_scale = jnp.exp(math.log(3.0) * jax.random.uniform(key_cols, (1, 1, 1, 1, COLS), jnp.float32))
    owners = N_SECTION * N_DP
    owner_ramp = jnp.exp(math.log(3.0) * jnp.arange(owners, dtype=jnp.float32) / max(owners - 1, 1))
    owner_ramp = owner_ramp.reshape(1, N_SECTION, N_DP, 1, 1)
    return 0.02 * base * row_scale * col_scale * owner_ramp


def strengthened(values, key, source, target, blocks, factor):
    owner, partner = [(jnp.arange(values.shape[position]) // (values.shape[position] // blocks)).reshape([-1 if axis == position else 1 for axis in range(values.ndim)]) for position in (source, target)]
    chosen = jax.random.permutation(key, blocks)[partner]
    strong = (owner == chosen) | (owner == (partner + blocks // 2) % blocks)
    return jnp.where(strong, factor * values, values)


def level_of(key, extent, shards, low, top_value):
    level = 1.0
    for dim, parts in shards:
        heights = jax.random.uniform(jax.random.fold_in(jax.random.fold_in(key, 6), dim), (parts,), jnp.float32, low / len(shards), top_value / len(shards))
        level = level * jnp.repeat(jnp.exp(heights), extent[dim] // parts).reshape((-1,) + (1,) * (len(extent) - 1 - dim))
    return level


def centred(stream_key, shape, width, bound, cuts=(), kind=jnp.bfloat16):
    factor_of = level_of(stream_key, shape, cuts, -0.22, 0.18) if cuts else 1.0
    array = jax.random.normal(stream_key, shape, jnp.float32) * width * factor_of
    return jnp.minimum(jnp.maximum(array, -bound), bound).astype(kind)


def gaussian_with(rng, extent, width, bound, cuts, heavy, kind=jnp.bfloat16):
    entries = width * jax.random.normal(rng, extent, jnp.float32)
    if cuts:
        entries = entries * level_of(rng, extent, cuts, -0.22, 0.18)
    return jnp.clip(strengthened(entries, jax.random.fold_in(rng, 3), *heavy), -bound, bound).astype(kind)


def setup_inputs(seed: int = 0) -> dict:
    arg_keys = jax.random.split(jax.random.key(seed), 9)
    return {
        "grad_mat": gaussian_with(arg_keys[0], (N_DP, N_TENSOR, D, COLS), 1.0, 6.0, ((0, 4), (1, 4), (2, 2)), (0, 2, 4, 2.0)),
        "grad_vec": gaussian_with(arg_keys[1], (N_DP, VECTOR), 1.0, 6.0, ((0, 4),), (0, 1, 4, 2.0)),
        "master_mat": draw_master_mat(jax.random.fold_in(arg_keys[8], 71), 0),
        "first_mat": centred(arg_keys[3], (N_TENSOR, N_SECTION, N_DP, OWNED_ROWS, COLS), 0.3, 4.0, ((0, 4), (1, 2), (2, 4)), jnp.float32),
        "second_mat": jnp.clip(jnp.exp(math.log(0.1) - 4.6051702 * jax.random.uniform(arg_keys[4], (N_TENSOR, N_SECTION, N_DP, OWNED_ROWS, COLS), jnp.float32) ** level_of(arg_keys[4], (N_TENSOR, N_SECTION, N_DP, OWNED_ROWS, COLS), ((0, 4), (1, 2), (2, 4)), -0.2, 0.2)), 0.001, 0.1),
        "master_vec": centred(arg_keys[5], (N_DP, OWNED_VECTOR), 1.0, 6.0, ((0, 4),), jnp.float32),
        "first_vec": centred(arg_keys[6], (N_DP, OWNED_VECTOR), 0.3, 4.0, ((0, 4),), jnp.float32),
        "second_vec": jnp.clip(jnp.exp(math.log(0.1) - 4.6051702 * jax.random.uniform(arg_keys[7], (N_DP, OWNED_VECTOR), jnp.float32) ** level_of(arg_keys[7], (N_DP, OWNED_VECTOR), ((0, 4),), -0.2, 0.2)), 0.001, 0.1),
    }


BETA_ONE = 0.9
BETA_TWO = 0.999
EPSILON = 1e-06
LEARN_RATE = 0.25
DECAY_MAT = 0.01

def adam_direction(gradient, master, first, second, decay):
    first_new = BETA_ONE * first + (1.0 - BETA_ONE) * gradient
    second_new = BETA_TWO * second + (1.0 - BETA_TWO) * gradient * gradient
    corr_one = 1.0 - BETA_ONE ** STEP
    corr_two = 1.0 - BETA_TWO ** STEP
    direction = first_new / corr_one / (jnp.sqrt(second_new / corr_two) + EPSILON) + decay * master
    return (first_new, second_new, direction)

def segment_ratio(weight_cols, update_cols, bounds):
    pieces = []
    for index in range(len(bounds) - 1):
        lower = bounds[index]
        upper = bounds[index + 1]
        ratio = jnp.sqrt(jnp.sum(weight_cols[lower:upper])) / jnp.sqrt(jnp.sum(update_cols[lower:upper]))
        pieces.append(jnp.full((upper - lower,), ratio, dtype=weight_cols.dtype))
    return jnp.concatenate(pieces)

def reference(grad_mat, grad_vec, master_mat, first_mat, second_mat, master_vec, first_vec, second_vec):
    tensor_count = N_TENSOR
    columns = (4 * D + 2 * FF) // tensor_count
    state_shape = master_mat.shape
    gradient = lax.optimization_barrier(jnp.sum(grad_mat, axis=0, dtype=jnp.float32))
    master = master_mat.reshape(tensor_count, D, columns)
    first = first_mat.reshape(tensor_count, D, columns)
    second = second_mat.reshape(tensor_count, D, columns)
    first_new, second_new, direction = adam_direction(gradient, master, first, second, DECAY_MAT)
    bounds_mat = [0, 3 * D // tensor_count, 4 * D // tensor_count, (4 * D + FF) // tensor_count, columns]
    weight_cols = lax.optimization_barrier(jnp.sum(master * master, axis=(0, 1)))
    update_cols = lax.optimization_barrier(jnp.sum(direction * direction, axis=(0, 1)))
    ratio_cols = segment_ratio(weight_cols, update_cols, bounds_mat)
    master_new = master - LEARN_RATE * ratio_cols * direction
    length = 9 * D + FF
    vec_shape = master_vec.shape
    gradient_vec = lax.optimization_barrier(jnp.sum(grad_vec, axis=0, dtype=jnp.float32))
    master_v = master_vec.reshape(length)
    first_v, second_v, direction_v = adam_direction(gradient_vec, master_v, first_vec.reshape(length), second_vec.reshape(length), 0.0)
    bounds_vec = [0, D, 2 * D, 5 * D, 6 * D, 7 * D, 8 * D, 8 * D + FF, 9 * D + FF]
    ratio_vec = segment_ratio(master_v * master_v, direction_v * direction_v, bounds_vec)
    master_v_new = master_v - LEARN_RATE * ratio_vec * direction_v
    return (master_new.astype(jnp.bfloat16), master_v_new.astype(jnp.bfloat16), master_new.reshape(state_shape), first_new.reshape(state_shape), second_new.reshape(state_shape), master_v_new.reshape(vec_shape), first_v.reshape(vec_shape), second_v.reshape(vec_shape))
```

```python
import functools

import jax
import jax.numpy as jnp
from jax import lax
from jax.experimental import pallas as pl
from jax.experimental.pallas import tpu as pltpu
from jax.sharding import PartitionSpec as P

D = 1600
FF = 6400
STEP = 10

BETA_ONE = 0.9
BETA_TWO = 0.999
EPSILON = 1e-06
LEARN_RATE = 0.25
DECAY_MAT = 0.01
LANES = 128
MESH = pl.DeviceIdType.MESH
GROUPS = ((3,), (2,), (0,), (1,))
AHEAD = 2


def adam_direction(gradient, master, first, second, decay):
    first_new = BETA_ONE * first + (1.0 - BETA_ONE) * gradient
    second_new = BETA_TWO * second + (1.0 - BETA_TWO) * gradient * gradient
    corr_one = 1.0 - BETA_ONE**STEP
    corr_two = 1.0 - BETA_TWO**STEP
    direction = first_new * (1.0 / corr_one) / (jnp.sqrt(second_new * (1.0 / corr_two)) + EPSILON)
    if decay:
        direction = direction + decay * master
    return (first_new, second_new, direction)


def plan(bounds, columns):
    tiles = -(-columns // LANES)

    def touched(group):
        found = set()
        for p in group:
            found |= set(range(bounds[p] // LANES, -(-bounds[p + 1] // LANES)))
        return found

    def ranges(found):
        out = []
        for t in sorted(found):
            if out and out[-1][1] == t:
                out[-1][1] = t + 1
            else:
                out.append([t, t + 1])
        return [(a * LANES, min(b * LANES, columns)) for a, b in out]

    reduced, seen = [], set()
    for group in GROUPS:
        reduced.append(ranges(touched(group) - seen))
        seen |= touched(group)
    assert len(seen) == tiles
    gathered, seen = [], set()
    for group in reversed(GROUPS):
        gathered.insert(0, ranges(touched(group) - seen))
        seen |= touched(group)
    return reduced, gathered


def over_tiles(lo, hi, body):
    full = (hi - lo) // LANES

    def step(j, carry):
        body(pl.ds(pl.multiple_of(lo + j * LANES, LANES), LANES), lo + j * LANES, LANES)
        return carry

    lax.fori_loop(0, full, step, 0)
    rest = hi - lo - full * LANES
    if rest:
        body(pl.ds(lo + full * LANES, rest), lo + full * LANES, rest)


def kernel(
    n, tensors, sections, bounds, bounds_vec, reduced, gathered,
    grad, gvec, mat_m, mat_f, mat_s, vec_m, vec_f, vec_s,
    out_w, out_m, out_f, out_s, out_gv, out_vm, out_vf, out_vs,
    got, own, master, first, second, direc, weights, csum_w, csum_u, vgot, vall, pmsg, pgot, dmsg, dgot,
    load_sem, rs_send, rs_recv, vs_send, vs_recv, vg_send, vg_recv, p_send, p_recv, d_send, d_recv,
    ag_send, ag_recv, out_sem, own_sem,
):
    me = lax.axis_index("dp")
    tensor, section = lax.axis_index("tensor"), lax.axis_index("section")
    groups = len(GROUPS)
    plane = tensors * sections
    spot = tensor * sections + section
    columns = own.shape[1]
    owned_vec = vec_m.shape[1]

    loads = [
        pltpu.make_async_copy(src, dst, load_sem.at[i])
        for i, (src, dst) in enumerate(((grad.at[me], own), (mat_m, master), (mat_f, first), (mat_s, second)))
    ]
    for load in loads:
        load.start()

    dp_peers = [{"dp": lax.rem(me + d, n)} for d in range(1, n)]
    plane_peers = []
    for d in range(1, plane):
        other = lax.rem(spot + d, plane)
        plane_peers.append({"tensor": other // sections, "section": lax.rem(other, sections)})
    barrier = pltpu.get_barrier_semaphore()
    for peer in dp_peers + plane_peers:
        pl.semaphore_signal(barrier, inc=1, device_id=peer, device_id_type=MESH)
    pl.semaphore_wait(barrier, len(dp_peers) + len(plane_peers))

    def remote(src, dst, send, recv, peer):
        return pltpu.make_async_remote_copy(
            src_ref=src, dst_ref=dst, send_sem=send, recv_sem=recv, device_id=peer, device_id_type=MESH
        )

    rs_index = []
    for g in range(groups):
        for k in range(len(reduced[g])):
            rs_index.append((g, k))
    ag_index = []
    for g in range(groups):
        for k in range(len(gathered[g])):
            ag_index.append((g, k))

    def rs_copies(g):
        copies = []
        for k, (lo, hi) in enumerate(reduced[g]):
            i = rs_index.index((g, k))
            for d in range(1, n):
                peer = dp_peers[d - 1]
                cols = pl.ds(lo, hi - lo)
                copies.append(remote(
                    grad.at[peer["dp"], :, cols], got.at[d - 1, :, cols],
                    rs_send.at[i, d - 1], rs_recv.at[i, d - 1], peer,
                ))
        return copies

    vec_copies = [
        remote(gvec.at[peer["dp"]], vgot.at[d], vs_send.at[d], vs_recv.at[d], peer) for d, peer in enumerate(dp_peers)
    ]
    for copy in vec_copies:
        copy.start()
    for g in range(min(AHEAD, groups)):
        for copy in rs_copies(g):
            copy.start()
    for load in loads:
        load.wait()

    vall_copies = [
        remote(vall.at[me], vall.at[me], vg_send.at[d], vg_recv.at[d], peer) for d, peer in enumerate(dp_peers)
    ]
    outs = []
    ratios = {}
    row = lax.broadcasted_iota(jnp.int32, (8, LANES), 0)
    lane = lax.broadcasted_iota(jnp.int32, (8, LANES), 1)

    def put(block, slot, weight_sq, update_sq):
        block = jnp.where((row == 0) & (lane == slot), weight_sq, block)
        return jnp.where((row == 1) & (lane == slot), update_sq, block)

    def pick(ratio, slot):
        return jnp.sum(jnp.where(lane[0:1] == slot, ratio, 0.0), axis=1, keepdims=True)

    def keep(src, dst):
        copy = pltpu.make_async_copy(src, dst, out_sem.at[len(outs)])
        copy.start()
        outs.append(copy)

    def hop(g, step, way, source, received):
        copies = []
        shard = source - step if way == 0 else source + step
        to = me + 1 if way == 0 else me - 1
        to = jnp.clip(to, 0, n - 1)
        shard = jnp.clip(shard, 0, n - 1)
        for k, (lo, hi) in enumerate(gathered[g]):
            i = ag_index.index((g, k))
            cols = pl.ds(lo, hi - lo)
            dst = out_w.at[shard, :, cols]
            src = weights.at[:, cols] if step == 0 and not received else dst
            copies.append(remote(src, dst, ag_send.at[i, way, step], ag_recv.at[i, way, step], {"dp": to}))
        return copies

    def leaving(step, way):
        if way == 0:
            return (me < n - 1) & (me >= step)
        return (me > 0) & (me + step <= n - 1)

    def reaching(step, way):
        if way == 0:
            return me - 1 - step >= 0
        return me + 1 + step <= n - 1

    def send_hop(g, step):
        for way in (0, 1):
            if step:
                @pl.when(reaching(step - 1, way))
                def _():
                    for copy in hop(g, step - 1, way, me - 1 if way == 0 else me + 1, True):
                        copy.wait_recv()
            if step < n - 1:
                @pl.when(leaving(step, way))
                def _():
                    for copy in hop(g, step, way, me, False):
                        copy.start()

    hops_done = [0] * groups

    def advance(g):
        if hops_done[g] <= n - 1:
            send_hop(g, hops_done[g])
            hops_done[g] += 1

    for g in range(groups):
        for copy in rs_copies(g):
            copy.wait()
        if g + AHEAD < groups:
            for copy in rs_copies(g + AHEAD):
                copy.start()
        for lo, hi in reduced[g]:
            def reduce_tile(cols, start, width):
                total = own[:, cols].astype(jnp.float32)
                for d in range(n - 1):
                    total = total + got[d, :, cols].astype(jnp.float32)
                old = master[:, cols]
                first_new, second_new, update = adam_direction(total, old, first[:, cols], second[:, cols], DECAY_MAT)
                first[:, cols] = first_new
                second[:, cols] = second_new
                direc[:, cols] = update
                csum_w[:, cols] = jnp.sum(old * old, axis=0, keepdims=True)
                csum_u[:, cols] = jnp.sum(update * update, axis=0, keepdims=True)

            over_tiles(lo, hi, reduce_tile)
        block = jnp.zeros((8, LANES), jnp.float32)
        column = lax.broadcasted_iota(jnp.int32, (1, columns), 1)
        for p in GROUPS[g]:
            inside = (column >= bounds[p]) & (column < bounds[p + 1])
            block = put(
                block, p,
                jnp.sum(jnp.where(inside, csum_w[...], 0.0), axis=1, keepdims=True),
                jnp.sum(jnp.where(inside, csum_u[...], 0.0), axis=1, keepdims=True),
            )
        pmsg[g] = block
        plane_copies = [
            remote(pmsg.at[g], pgot.at[g, d], p_send.at[g, d], p_recv.at[g, d], peer)
            for d, peer in enumerate(plane_peers)
        ]
        for copy in plane_copies:
            copy.start()
        for lo, hi in reduced[g]:
            cols = pl.ds(lo, hi - lo)
            keep(first.at[:, cols], out_f.at[:, cols])
            keep(second.at[:, cols], out_s.at[:, cols])
        if g == 0:
            for copy in vec_copies:
                copy.wait()
            total_v = gvec[me]
            for d in range(n - 1):
                total_v = total_v + vgot[d]
            old_v = vec_m[...]
            first_v, second_v, update_v = adam_direction(total_v, old_v, vec_f[...], vec_s[...], 0.0)
            out_vf[...] = first_v
            out_vs[...] = second_v
            index = me * owned_vec + lax.broadcasted_iota(jnp.int32, (1, owned_vec), 1)
            extra = jnp.zeros((8, LANES), jnp.float32)
            for p in range(len(bounds_vec) - 1):
                inside = (index >= bounds_vec[p]) & (index < bounds_vec[p + 1])
                extra = put(
                    extra, 4 + p,
                    jnp.sum(jnp.where(inside, old_v * old_v, 0.0), axis=1, keepdims=True),
                    jnp.sum(jnp.where(inside, update_v * update_v, 0.0), axis=1, keepdims=True),
                )
        for d, copy in enumerate(plane_copies):
            copy.wait()
            block = block + pgot[g, d]
        if g == 0:
            block = block + extra
        dmsg[g] = block
        dp_copies = [
            remote(dmsg.at[g], dgot.at[g, d], d_send.at[g, d], d_recv.at[g, d], peer) for d, peer in enumerate(dp_peers)
        ]
        for copy in dp_copies:
            copy.start()
        for earlier in range(g):
            advance(earlier)
        for d, copy in enumerate(dp_copies):
            copy.wait()
            block = block + dgot[g, d]
        ratio = jnp.sqrt(block[0:1]) / jnp.sqrt(block[1:2])
        for p in GROUPS[g]:
            ratios[p] = LEARN_RATE * pick(ratio, p)
        for lo, hi in gathered[g]:
            def apply_tile(cols, start, width):
                position = start + lax.broadcasted_iota(jnp.int32, (1, width), 1)
                scale = jnp.zeros((1, width), jnp.float32)
                for p, value in ratios.items():
                    scale = jnp.where((position >= bounds[p]) & (position < bounds[p + 1]), value, scale)
                new = master[:, cols] - scale * direc[:, cols]
                master[:, cols] = new
                weights[:, cols] = new.astype(jnp.bfloat16)

            over_tiles(lo, hi, apply_tile)
        advance(g)
        for k, (lo, hi) in enumerate(gathered[g]):
            cols = pl.ds(lo, hi - lo)
            keep(weights.at[:, cols], out_w.at[me, :, cols])
            keep(master.at[:, cols], out_m.at[:, cols])
        if g == 0:
            scale_v = jnp.zeros((1, owned_vec), jnp.float32)
            for p in range(len(bounds_vec) - 1):
                inside = (index >= bounds_vec[p]) & (index < bounds_vec[p + 1])
                scale_v = jnp.where(inside, LEARN_RATE * pick(ratio, 4 + p), scale_v)
            new_v = old_v - scale_v * update_v
            out_vm[...] = new_v
            vall[me] = new_v
            for copy in vall_copies:
                copy.start()
    for _ in range(n):
        for g in range(groups):
            advance(g)
    for d, copy in enumerate(vall_copies):
        copy.wait_send()
        origin = lax.rem(me + n - 1 - d, n)
        remote(vall.at[origin], vall.at[origin], vg_send.at[d], vg_recv.at[d], dp_peers[d]).wait_recv()
    out_gv[...] = vall[...]
    for g in range(groups):
        for step in range(n - 1):
            for way in (0, 1):
                @pl.when(leaving(step, way))
                def _():
                    for copy in hop(g, step, way, me, False):
                        copy.wait_send()
    for copy in outs:
        copy.wait()


def local(grad_mat, grad_vec, master_mat, first_mat, second_mat, master_vec, first_vec, second_vec):
    n, tensors, sections = (lax.axis_size(name) for name in ("dp", "tensor", "section"))
    section_rows, columns = grad_mat.shape[2:]
    rows = section_rows // n
    state_shape = master_mat.shape
    owned_vec = master_vec.shape[1]
    bounds = (0, 3 * D // tensors, 4 * D // tensors, (4 * D + FF) // tensors, columns)
    bounds_vec = (0, D, 2 * D, 5 * D, 6 * D, 7 * D, 8 * D, 8 * D + FF, 9 * D + FF)
    reduced, gathered = plan(bounds, columns)
    groups = len(GROUPS)
    n_rs, n_ag = sum(map(len, reduced)), sum(map(len, gathered))
    plane = tensors * sections
    f32, bf16 = jnp.float32, jnp.bfloat16
    any_space, vmem = pl.BlockSpec(memory_space=pl.ANY), pl.BlockSpec(memory_space=pltpu.VMEM)
    dma = pltpu.SemaphoreType.DMA
    mat = jax.ShapeDtypeStruct((rows, columns), f32)
    vec = jax.ShapeDtypeStruct((1, owned_vec), f32)
    weights, new_m, new_f, new_s, gathered_v, new_vm, new_vf, new_vs = pl.pallas_call(
        functools.partial(kernel, n, tensors, sections, bounds, bounds_vec, reduced, gathered),
        out_shape=[
            jax.ShapeDtypeStruct((n, rows, columns), bf16), mat, mat, mat,
            jax.ShapeDtypeStruct((n, 1, owned_vec), f32), vec, vec, vec,
        ],
        in_specs=[any_space, vmem, any_space, any_space, any_space, vmem, vmem, vmem],
        out_specs=[any_space, any_space, any_space, any_space, vmem, vmem, vmem, vmem],
        scratch_shapes=[
            pltpu.VMEM((n - 1, rows, columns), bf16),
            pltpu.VMEM((rows, columns), bf16),
            pltpu.VMEM((rows, columns), f32),
            pltpu.VMEM((rows, columns), f32),
            pltpu.VMEM((rows, columns), f32),
            pltpu.VMEM((rows, columns), f32),
            pltpu.VMEM((rows, columns), bf16),
            pltpu.VMEM((1, columns), f32),
            pltpu.VMEM((1, columns), f32),
            pltpu.VMEM((n - 1, 1, owned_vec), f32),
            pltpu.VMEM((n, 1, owned_vec), f32),
            pltpu.VMEM((groups, 8, LANES), f32),
            pltpu.VMEM((groups, plane - 1, 8, LANES), f32),
            pltpu.VMEM((groups, 8, LANES), f32),
            pltpu.VMEM((groups, n - 1, 8, LANES), f32),
            dma((4,)), dma((n_rs, n - 1)), dma((n_rs, n - 1)), dma((n - 1,)), dma((n - 1,)), dma((n - 1,)),
            dma((n - 1,)), dma((groups, plane - 1)), dma((groups, plane - 1)), dma((groups, n - 1)),
            dma((groups, n - 1)), dma((n_ag, 2, n - 1)), dma((n_ag, 2, n - 1)), dma((2 * n_rs + 2 * n_ag,)), dma((1,)),
        ],
        compiler_params=pltpu.CompilerParams(collective_id=0, has_side_effects=True, vmem_limit_bytes=56 << 20),
        cost_estimate=pl.CostEstimate(flops=40 * rows * columns, bytes_accessed=36 * rows * columns, transcendentals=0),
    )(
        grad_mat.reshape(n, rows, columns),
        grad_vec.astype(f32).reshape(n, 1, owned_vec),
        master_mat.reshape(rows, columns),
        first_mat.reshape(rows, columns),
        second_mat.reshape(rows, columns),
        master_vec, first_vec, second_vec,
    )
    return (
        weights.reshape(1, section_rows, columns),
        gathered_v.reshape(n * owned_vec).astype(bf16),
        new_m.reshape(state_shape),
        new_f.reshape(state_shape),
        new_s.reshape(state_shape),
        new_vm, new_vf, new_vs,
    )


def solution(mesh):
    state = P("tensor", "section", "dp", None, None)
    in_specs = (
        P("dp", "tensor", "section", None), P("dp", None), state, state, state, P("dp", None), P("dp", None), P("dp", None),
    )
    out_specs = (
        P("tensor", "section", None), P(), state, state, state, P("dp", None), P("dp", None), P("dp", None),
    )
    return jax.shard_map(local, mesh=mesh, in_specs=in_specs, out_specs=out_specs, check_vma=False)
```

```python
import functools

import jax
import jax.numpy as jnp
from jax import lax
from jax.experimental import pallas as pl
from jax.experimental.pallas import tpu as pltpu
from jax.sharding import PartitionSpec as P

D = 1600
FF = 6400
STEP = 10

BETA_ONE = 0.9
BETA_TWO = 0.999
EPSILON = 1e-06
LEARN_RATE = 0.25
DECAY_MAT = 0.01
LANES = 128
MESH = pl.DeviceIdType.MESH
GROUPS = ((0,), (3,), (2,), (1,))
PIECE = 3
AHEAD = 2
PART = 4


def adam_direction(gradient, master, first, second, decay):
    first_new = BETA_ONE * first + (1.0 - BETA_ONE) * gradient
    second_new = BETA_TWO * second + (1.0 - BETA_TWO) * gradient * gradient
    corr_one = 1.0 - BETA_ONE**STEP
    corr_two = 1.0 - BETA_TWO**STEP
    direction = first_new * (1.0 / corr_one) / (jnp.sqrt(second_new * (1.0 / corr_two)) + EPSILON)
    if decay:
        direction = direction + decay * master
    return (first_new, second_new, direction)


def plan(bounds, columns):
    tiles = -(-columns // LANES)

    def touched(group):
        found = set()
        for p in group:
            found |= set(range(bounds[p] // LANES, -(-bounds[p + 1] // LANES)))
        return found

    def ranges(found):
        out = []
        for t in sorted(found):
            if out and out[-1][1] == t:
                out[-1][1] = t + 1
            else:
                out.append([t, t + 1])
        return [(a * LANES, min(b * LANES, columns)) for a, b in out]

    def cut(found, size):
        out = []
        for lo, hi in ranges(found):
            count = -(-(hi - lo) // (size * LANES))
            step = -(-(hi - lo) // (count * LANES)) * LANES
            out += [(a, min(a + step, hi)) for a in range(lo, hi, step)]
        return out

    reduced, seen = [], set()
    for group in GROUPS:
        reduced.append(cut(touched(group) - seen, PIECE))
        seen |= touched(group)
    assert len(seen) == tiles
    gathered, seen = [], set()
    for group in reversed(GROUPS):
        gathered.insert(0, cut(touched(group) - seen, PART))
        seen |= touched(group)
    return reduced, gathered


def over_tiles(lo, hi, body):
    full = (hi - lo) // LANES

    def step(j, carry):
        body(pl.ds(pl.multiple_of(lo + j * LANES, LANES), LANES), lo + j * LANES, LANES)
        return carry

    lax.fori_loop(0, full, step, 0)
    rest = hi - lo - full * LANES
    if rest:
        body(pl.ds(lo + full * LANES, rest), lo + full * LANES, rest)


def kernel(
    n, tensors, sections, bounds, bounds_vec, reduced, gathered,
    grad, gvec, mat_m, mat_f, mat_s, vec_m, vec_f, vec_s,
    out_w, out_m, out_f, out_s, out_gv, out_vm, out_vf, out_vs,
    got, own, master, first, second, direc, weights, csum_w, csum_u, vgot, vall, pmsg, pgot, dmsg, dgot,
    load_sem, rs_send, rs_recv, vs_send, vs_recv, vg_send, vg_recv, p_send, p_recv, d_send, d_recv,
    ag_send, ag_recv, out_sem, own_sem,
):
    me = lax.axis_index("dp")
    tensor, section = lax.axis_index("tensor"), lax.axis_index("section")
    groups = len(GROUPS)
    plane = tensors * sections
    spot = tensor * sections + section
    columns = own.shape[1]
    owned_vec = vec_m.shape[1]

    loads = [
        pltpu.make_async_copy(src, dst, load_sem.at[i])
        for i, (src, dst) in enumerate(((grad.at[me], own), (mat_m, master), (mat_f, first), (mat_s, second)))
    ]
    for load in loads:
        load.start()

    dp_peers = [{"dp": lax.rem(me + d, n)} for d in range(1, n)]
    plane_peers = []
    for d in range(1, plane):
        other = lax.rem(spot + d, plane)
        plane_peers.append({"tensor": other // sections, "section": lax.rem(other, sections)})
    barrier = pltpu.get_barrier_semaphore()
    for peer in dp_peers + plane_peers:
        pl.semaphore_signal(barrier, inc=1, device_id=peer, device_id_type=MESH)
    pl.semaphore_wait(barrier, len(dp_peers) + len(plane_peers))

    def remote(src, dst, send, recv, peer):
        return pltpu.make_async_remote_copy(
            src_ref=src, dst_ref=dst, send_sem=send, recv_sem=recv, device_id=peer, device_id_type=MESH
        )

    pieces = [(g, lo, hi) for g in range(groups) for lo, hi in reduced[g]]
    parts = [(g, lo, hi) for g in range(groups) for lo, hi in gathered[g]]

    def rs_copies(i):
        _, lo, hi = pieces[i]
        cols = pl.ds(lo, hi - lo)
        return [
            remote(
                grad.at[peer["dp"], :, cols], got.at[d, :, cols], rs_send.at[i, d], rs_recv.at[i, d], peer
            )
            for d, peer in enumerate(dp_peers)
        ]

    vec_copies = [
        remote(gvec.at[peer["dp"]], vgot.at[d], vs_send.at[d], vs_recv.at[d], peer) for d, peer in enumerate(dp_peers)
    ]
    for copy in vec_copies:
        copy.start()
    for i in range(min(AHEAD, len(pieces))):
        for copy in rs_copies(i):
            copy.start()
    for load in loads:
        load.wait()

    vall_copies = [
        remote(vall.at[me], vall.at[me], vg_send.at[d], vg_recv.at[d], peer) for d, peer in enumerate(dp_peers)
    ]
    outs = []
    ratios = {}
    row = lax.broadcasted_iota(jnp.int32, (8, LANES), 0)
    lane = lax.broadcasted_iota(jnp.int32, (8, LANES), 1)

    def put(block, slot, weight_sq, update_sq):
        block = jnp.where((row == 0) & (lane == slot), weight_sq, block)
        return jnp.where((row == 1) & (lane == slot), update_sq, block)

    def pick(ratio, slot):
        return jnp.sum(jnp.where(lane[0:1] == slot, ratio, 0.0), axis=1, keepdims=True)

    def keep(src, dst):
        copy = pltpu.make_async_copy(src, dst, out_sem.at[len(outs)])
        copy.start()
        outs.append(copy)

    def hop(i, step, way, source, received):
        shard = source - step if way == 0 else source + step
        to = me + 1 if way == 0 else me - 1
        to = jnp.clip(to, 0, n - 1)
        shard = jnp.clip(shard, 0, n - 1)
        _, lo, hi = parts[i]
        cols = pl.ds(lo, hi - lo)
        dst = out_w.at[shard, :, cols]
        src = weights.at[:, cols] if step == 0 and not received else dst
        return remote(src, dst, ag_send.at[i, way, step], ag_recv.at[i, way, step], {"dp": to})

    def leaving(step, way):
        if way == 0:
            return (me < n - 1) & (me >= step)
        return (me > 0) & (me + step <= n - 1)

    def reaching(step, way):
        if way == 0:
            return me - 1 - step >= 0
        return me + 1 + step <= n - 1

    def send_hop(i, step):
        for way in (0, 1):
            if step:
                @pl.when(reaching(step - 1, way))
                def _():
                    hop(i, step - 1, way, me - 1 if way == 0 else me + 1, True).wait_recv()
            if step < n - 1:
                @pl.when(leaving(step, way))
                def _():
                    hop(i, step, way, me, False).start()

    hops_done = {}

    def advance_all():
        for i in hops_done:
            if hops_done[i] < n:
                send_hop(i, hops_done[i])
                hops_done[i] += 1

    for number, (g, piece_lo, piece_hi) in enumerate(pieces):
        for copy in rs_copies(number):
            copy.wait()
        if number + AHEAD < len(pieces):
            for copy in rs_copies(number + AHEAD):
                copy.start()
        for lo, hi in ((piece_lo, piece_hi),):
            def reduce_tile(cols, start, width):
                total = own[:, cols].astype(jnp.float32)
                for d in range(n - 1):
                    total = total + got[d, :, cols].astype(jnp.float32)
                old = master[:, cols]
                first_new, second_new, update = adam_direction(total, old, first[:, cols], second[:, cols], DECAY_MAT)
                first[:, cols] = first_new
                second[:, cols] = second_new
                direc[:, cols] = update
                csum_w[:, cols] = jnp.sum(old * old, axis=0, keepdims=True)
                csum_u[:, cols] = jnp.sum(update * update, axis=0, keepdims=True)

            over_tiles(lo, hi, reduce_tile)
            cols = pl.ds(lo, hi - lo)
            keep(first.at[:, cols], out_f.at[:, cols])
            keep(second.at[:, cols], out_s.at[:, cols])
        if number + 1 < len(pieces) and pieces[number + 1][0] == g:
            advance_all()
            continue
        block = jnp.zeros((8, LANES), jnp.float32)
        column = lax.broadcasted_iota(jnp.int32, (1, columns), 1)
        for p in GROUPS[g]:
            inside = (column >= bounds[p]) & (column < bounds[p + 1])
            block = put(
                block, p,
                jnp.sum(jnp.where(inside, csum_w[...], 0.0), axis=1, keepdims=True),
                jnp.sum(jnp.where(inside, csum_u[...], 0.0), axis=1, keepdims=True),
            )
        pmsg[g] = block
        plane_copies = [
            remote(pmsg.at[g], pgot.at[g, d], p_send.at[g, d], p_recv.at[g, d], peer)
            for d, peer in enumerate(plane_peers)
        ]
        for copy in plane_copies:
            copy.start()
        if g == 0:
            for copy in vec_copies:
                copy.wait()
            total_v = gvec[me]
            for d in range(n - 1):
                total_v = total_v + vgot[d]
            old_v = vec_m[...]
            first_v, second_v, update_v = adam_direction(total_v, old_v, vec_f[...], vec_s[...], 0.0)
            out_vf[...] = first_v
            out_vs[...] = second_v
            index = me * owned_vec + lax.broadcasted_iota(jnp.int32, (1, owned_vec), 1)
            extra = jnp.zeros((8, LANES), jnp.float32)
            for p in range(len(bounds_vec) - 1):
                inside = (index >= bounds_vec[p]) & (index < bounds_vec[p + 1])
                extra = put(
                    extra, 4 + p,
                    jnp.sum(jnp.where(inside, old_v * old_v, 0.0), axis=1, keepdims=True),
                    jnp.sum(jnp.where(inside, update_v * update_v, 0.0), axis=1, keepdims=True),
                )
        for d, copy in enumerate(plane_copies):
            copy.wait()
            block = block + pgot[g, d]
        if g == 0:
            block = block + extra
        dmsg[g] = block
        dp_copies = [
            remote(dmsg.at[g], dgot.at[g, d], d_send.at[g, d], d_recv.at[g, d], peer) for d, peer in enumerate(dp_peers)
        ]
        for copy in dp_copies:
            copy.start()
        advance_all()
        for d, copy in enumerate(dp_copies):
            copy.wait()
            block = block + dgot[g, d]
        ratio = jnp.sqrt(block[0:1]) / jnp.sqrt(block[1:2])
        for p in GROUPS[g]:
            ratios[p] = LEARN_RATE * pick(ratio, p)
        for lo, hi in gathered[g]:
            def apply_tile(cols, start, width):
                position = start + lax.broadcasted_iota(jnp.int32, (1, width), 1)
                scale = jnp.zeros((1, width), jnp.float32)
                for p, value in ratios.items():
                    scale = jnp.where((position >= bounds[p]) & (position < bounds[p + 1]), value, scale)
                new = master[:, cols] - scale * direc[:, cols]
                master[:, cols] = new
                weights[:, cols] = new.astype(jnp.bfloat16)

            over_tiles(lo, hi, apply_tile)
            i = parts.index((g, lo, hi))
            send_hop(i, 0)
            hops_done[i] = 1
        for lo, hi in gathered[g]:
            cols = pl.ds(lo, hi - lo)
            keep(weights.at[:, cols], out_w.at[me, :, cols])
            keep(master.at[:, cols], out_m.at[:, cols])
        if g == 0:
            scale_v = jnp.zeros((1, owned_vec), jnp.float32)
            for p in range(len(bounds_vec) - 1):
                inside = (index >= bounds_vec[p]) & (index < bounds_vec[p + 1])
                scale_v = jnp.where(inside, LEARN_RATE * pick(ratio, 4 + p), scale_v)
            new_v = old_v - scale_v * update_v
            out_vm[...] = new_v
            vall[me] = new_v
            for copy in vall_copies:
                copy.start()
    for _ in range(n):
        advance_all()
    for d, copy in enumerate(vall_copies):
        copy.wait_send()
        origin = lax.rem(me + n - 1 - d, n)
        remote(vall.at[origin], vall.at[origin], vg_send.at[d], vg_recv.at[d], dp_peers[d]).wait_recv()
    out_gv[...] = vall[...]
    for i in range(len(parts)):
        for step in range(n - 1):
            for way in (0, 1):
                @pl.when(leaving(step, way))
                def _():
                    hop(i, step, way, me, False).wait_send()
    for copy in outs:
        copy.wait()


def hand_over(*refs):
    count = (len(refs) - 2) // 3
    load_sem, store_sem = refs[-2:]
    loads, stores = [], []
    for i in range(count):
        src, dst, buf = refs[i], refs[count + i], refs[2 * count + i]
        total = src.shape[0]
        size = total if total < 16 else -(-total // (4 * 16)) * 16
        if src.dtype == jnp.bfloat16:
            size = 1
        for lo in range(0, total, size):
            part = pl.ds(lo, min(size, total - lo))
            k = len(loads)
            loads.append(pltpu.make_async_copy(src.at[part], buf.at[part], load_sem.at[k]))
            stores.append(pltpu.make_async_copy(buf.at[part], dst.at[part], store_sem.at[k]))
    for load in loads:
        load.start()
    for load, store in zip(loads, stores):
        load.wait()
        store.start()
    for store in stores:
        store.wait()


def local(grad_mat, grad_vec, master_mat, first_mat, second_mat, master_vec, first_vec, second_vec):
    n, tensors, sections = (lax.axis_size(name) for name in ("dp", "tensor", "section"))
    section_rows, columns = grad_mat.shape[2:]
    rows = section_rows // n
    state_shape = master_mat.shape
    owned_vec = master_vec.shape[1]
    bounds = (0, 3 * D // tensors, 4 * D // tensors, (4 * D + FF) // tensors, columns)
    bounds_vec = (0, D, 2 * D, 5 * D, 6 * D, 7 * D, 8 * D, 8 * D + FF, 9 * D + FF)
    reduced, gathered = plan(bounds, columns)
    groups = len(GROUPS)
    n_rs, n_ag = sum(map(len, reduced)), sum(map(len, gathered))
    plane = tensors * sections
    f32, bf16 = jnp.float32, jnp.bfloat16
    any_space, vmem = pl.BlockSpec(memory_space=pl.ANY), pl.BlockSpec(memory_space=pltpu.VMEM)
    dma = pltpu.SemaphoreType.DMA
    mat = jax.ShapeDtypeStruct((rows, columns), f32)
    vec = jax.ShapeDtypeStruct((1, owned_vec), f32)
    weights, new_m, new_f, new_s, gathered_v, new_vm, new_vf, new_vs = pl.pallas_call(
        functools.partial(kernel, n, tensors, sections, bounds, bounds_vec, reduced, gathered),
        out_shape=[
            jax.ShapeDtypeStruct((n, rows, columns), bf16), mat, mat, mat,
            jax.ShapeDtypeStruct((n, 1, owned_vec), f32), vec, vec, vec,
        ],
        in_specs=[any_space, vmem, any_space, any_space, any_space, vmem, vmem, vmem],
        out_specs=[any_space, any_space, any_space, any_space, vmem, vmem, vmem, vmem],
        scratch_shapes=[
            pltpu.VMEM((n - 1, rows, columns), bf16),
            pltpu.VMEM((rows, columns), bf16),
            pltpu.VMEM((rows, columns), f32),
            pltpu.VMEM((rows, columns), f32),
            pltpu.VMEM((rows, columns), f32),
            pltpu.VMEM((rows, columns), f32),
            pltpu.VMEM((rows, columns), bf16),
            pltpu.VMEM((1, columns), f32),
            pltpu.VMEM((1, columns), f32),
            pltpu.VMEM((n - 1, 1, owned_vec), f32),
            pltpu.VMEM((n, 1, owned_vec), f32),
            pltpu.VMEM((groups, 8, LANES), f32),
            pltpu.VMEM((groups, plane - 1, 8, LANES), f32),
            pltpu.VMEM((groups, 8, LANES), f32),
            pltpu.VMEM((groups, n - 1, 8, LANES), f32),
            dma((4,)), dma((n_rs, n - 1)), dma((n_rs, n - 1)), dma((n - 1,)), dma((n - 1,)), dma((n - 1,)),
            dma((n - 1,)), dma((groups, plane - 1)), dma((groups, plane - 1)), dma((groups, n - 1)),
            dma((groups, n - 1)), dma((n_ag, 2, n - 1)), dma((n_ag, 2, n - 1)), dma((2 * n_rs + 2 * n_ag,)), dma((1,)),
        ],
        compiler_params=pltpu.CompilerParams(collective_id=0, has_side_effects=True, vmem_limit_bytes=56 << 20),
        cost_estimate=pl.CostEstimate(flops=40 * rows * columns, bytes_accessed=36 * rows * columns, transcendentals=0),
    )(
        grad_mat.reshape(n, rows, columns),
        grad_vec.astype(f32).reshape(n, 1, owned_vec),
        master_mat.reshape(rows, columns),
        first_mat.reshape(rows, columns),
        second_mat.reshape(rows, columns),
        master_vec, first_vec, second_vec,
    )
    handed = (weights, new_m, new_f, new_s, new_vm, new_vf, new_vs)
    weights, new_m, new_f, new_s, new_vm, new_vf, new_vs = pl.pallas_call(
        hand_over,
        out_shape=[jax.ShapeDtypeStruct(a.shape, a.dtype) for a in handed],
        in_specs=[any_space] * len(handed),
        out_specs=[any_space] * len(handed),
        scratch_shapes=[pltpu.VMEM(a.shape, a.dtype) for a in handed] + [dma((n + 16,)), dma((n + 16,))],
        compiler_params=pltpu.CompilerParams(vmem_limit_bytes=60 << 20),
        cost_estimate=pl.CostEstimate(flops=0, bytes_accessed=40 * rows * columns, transcendentals=0),
    )(*handed)
    return (
        weights.reshape(1, section_rows, columns),
        gathered_v.reshape(n * owned_vec).astype(bf16),
        new_m.reshape(state_shape),
        new_f.reshape(state_shape),
        new_s.reshape(state_shape),
        new_vm, new_vf, new_vs,
    )


def solution(mesh):
    state = P("tensor", "section", "dp", None, None)
    in_specs = (
        P("dp", "tensor", "section", None), P("dp", None), state, state, state, P("dp", None), P("dp", None), P("dp", None),
    )
    out_specs = (
        P("tensor", "section", None), P(), state, state, state, P("dp", None), P("dp", None), P("dp", None),
    )
    return jax.shard_map(local, mesh=mesh, in_specs=in_specs, out_specs=out_specs, check_vma=False)
```
